32 devices in a mesh: dp: 16 (over z, x, core), shard: 2 (over y).
Axes of the slice: x: 2, y: 2, z: 4, core: 2. Of those that a mesh axis runs over, the one named last changes fastest.
Arguments:
- tokens: bfloat16 [4096, 1024], P(('dp', 'shard')), may hold values from -6 to 6
- cotangent: bfloat16 [4096, 1024], P(('dp', 'shard')), may hold values from -6 to 6
- assign: int32 [4096], P('dp'), may hold values from 0 to 1
- prob: float32 [4096], P('dp'), may hold values from 0.2 to 1
- w_gate: bfloat16 [2, 1024, 4096], P(None, None, 'shard'), may hold values from -0.1875 to 0.1875
- w_up: bfloat16 [2, 1024, 4096], P(None, None, 'shard'), may hold values from -0.1875 to 0.1875
- w_down: bfloat16 [2, 4096, 1024], P(None, 'shard'), may hold values from -0.09375 to 0.09375
Outputs:
- output: bfloat16 [4096, 1024], P(('dp', 'shard'))
- input_grad: bfloat16 [4096, 1024], P(('dp', 'shard'))
- grad_gate: float32 [2, 1024, 4096], P(None, 'dp', 'shard')
- grad_up: float32 [2, 1024, 4096], P(None, 'dp', 'shard')
- grad_down: float32 [2, 4096, 1024], P(None, 'shard', 'dp')
The draws below stay inside these ranges and needn't reach their ends.
All inputs are finite; a program needn't handle non-finite values.
Results may differ from the reference program's by a relative error of at most 0.0057.
Values may be sent and summed in bfloat16 or wider, within the bound.
A program may use at most 192 MiB of HBM per device.

```python
import jax
import jax.numpy as jnp
from jax import lax

D = 1024
FF = 4096
EXP = 2
BLOCK = 128
TOKENS = 4096


def plant(values, rng, least, top_value):
    longest = values.shape.index(max(values.shape))
    spots = []
    for shift in (0, 1):
        where = [jax.random.randint(jax.random.fold_in(rng, axis), (), 0, length) for axis, length in enumerate(values.shape)]
        where[longest] = (where[longest] + shift) % values.shape[longest]
        spots.append(tuple(where))
    return values.at[spots[0]].set(least).at[spots[1]].set(top_value)


def levels(own_key, shape, shards, low, high):
    def one(axis_at, parts):
        steps = jax.random.uniform(jax.random.fold_in(jax.random.fold_in(own_key, 6), axis_at), (parts,), jnp.float32, low / len(shards), high / len(shards))
        return jnp.repeat(jnp.exp(steps), shape[axis_at] // parts).reshape((-1,) + (1,) * (len(shape) - axis_at - 1))

    gain = one(*shards[0])
    for cut in shards[1:]:
        gain = gain * one(*cut)
    return gain


def scatter_about(key, dims, scale, bound, pieces=(), kind=jnp.bfloat16):
    level = levels(key, dims, pieces, -0.22, 0.18) if pieces else 1.0
    array = jax.random.normal(key, dims, jnp.float32) * scale * level
    return jnp.minimum(jnp.maximum(array, -bound), bound).astype(kind)


def setup_inputs(seed: int = 0) -> dict:
    arg_keys = jax.random.split(jax.random.key(seed), 8)
    tokens = scatter_about(arg_keys[0], (TOKENS, D), 1.0, 6.0, ((0, 32),))
    cotangent = scatter_about(arg_keys[1], (TOKENS, D), 1.0, 6.0, ((0, 32),))
    assign = plant(jax.random.randint(arg_keys[2], (TOKENS,), 0, EXP), jax.random.fold_in(arg_keys[2], 1), 0, EXP - 1).astype(jnp.int32)
    prob = jnp.clip(0.2 + 0.8 * jax.random.uniform(arg_keys[3], (TOKENS,), jnp.float32) ** levels(arg_keys[3], (TOKENS,), ((0, 16),), -0.2, 0.2), 0.2, 1.0)
    w_gate = scatter_about(arg_keys[4], (EXP, D, FF), D ** -0.5, 0.1875, ((2, 2),))
    w_up = scatter_about(arg_keys[5], (EXP, D, FF), D ** -0.5, 0.1875, ((2, 2),))
    w_down = scatter_about(arg_keys[6], (EXP, FF, D), FF ** -0.5, 0.09375, ((1, 2),))
    return {"tokens": tokens, "cotangent": cotangent, "assign": assign, "prob": prob, "w_gate": w_gate, "w_up": w_up, "w_down": w_down}


def arrange(assign, experts, block_rows):
    row_count = assign.shape[0]
    labels = jnp.arange(experts, dtype=jnp.int32)
    onehot = (assign[:, None] == labels[None, :]).astype(jnp.int32)
    counts = jnp.sum(onehot, axis=0).astype(jnp.int32)
    blocks = ((counts + block_rows - 1) // block_rows).astype(jnp.int32)
    block_ends = jnp.cumsum(blocks).astype(jnp.int32)
    firsts = block_ends - blocks
    before = (jnp.cumsum(onehot, axis=0) - onehot).astype(jnp.int32)
    rank_in = jnp.sum(onehot * before, axis=1).astype(jnp.int32)
    token_slot = (jnp.sum(onehot * (firsts * block_rows)[None, :], axis=1) + rank_in).astype(jnp.int32)
    nblocks = row_count // block_rows + experts - 1
    slot_token = jnp.zeros((nblocks * block_rows,), jnp.int32).at[token_slot].set(jnp.arange(row_count, dtype=jnp.int32))
    slot_live = jnp.zeros((nblocks * block_rows,), jnp.float32).at[token_slot].set(1.0)
    block_index = jnp.arange(nblocks, dtype=jnp.int32)
    block_expert = jnp.minimum(jnp.sum((block_ends[None, :] <= block_index[:, None]).astype(jnp.int32), axis=1), experts - 1).astype(jnp.int32)
    return token_slot, slot_token, slot_live, block_expert


def add_at(total, expert, term):
    old = lax.dynamic_index_in_dim(total, expert, 0, keepdims=True)
    return lax.dynamic_update_index_in_dim(total, old + term[None], expert, 0)


def reference(tokens, cotangent, assign, prob, w_gate, w_up, w_down):
    token_slot, slot_token, slot_live, block_expert = arrange(assign, EXP, BLOCK)
    nblocks = block_expert.shape[0]
    scaled_grad = (prob[:, None] * cotangent.astype(jnp.float32)).astype(jnp.bfloat16)
    width = tokens.shape[1]

    def one_block(carry, block_index):
        grad_gate, grad_up, grad_down = carry
        chosen = lax.dynamic_slice_in_dim(slot_token, block_index * BLOCK, BLOCK)
        live = lax.dynamic_slice_in_dim(slot_live, block_index * BLOCK, BLOCK)
        expert = block_expert[block_index]
        gate_w = lax.dynamic_index_in_dim(w_gate, expert, 0, keepdims=False)
        up_w = lax.dynamic_index_in_dim(w_up, expert, 0, keepdims=False)
        down_w = lax.dynamic_index_in_dim(w_down, expert, 0, keepdims=False)
        rows_x = jnp.where(live[:, None] > 0, tokens[chosen], jnp.zeros((), tokens.dtype))
        rows_dout = jnp.where(live[:, None] > 0, scaled_grad[chosen], jnp.zeros((), scaled_grad.dtype))
        slot_prob = prob[chosen] * live
        gate_act = jnp.dot(rows_x, gate_w, preferred_element_type=jnp.float32)
        up_act = jnp.dot(rows_x, up_w, preferred_element_type=jnp.float32)
        sigma = jax.nn.sigmoid(gate_act)
        hidden = (gate_act * sigma * up_act).astype(jnp.bfloat16)
        partial_out = jnp.dot(hidden, down_w, preferred_element_type=jnp.float32)
        back_hidden = jnp.dot(rows_dout, down_w.T, preferred_element_type=jnp.float32)
        gate_grad = (back_hidden * up_act * sigma * (1.0 + gate_act * (1.0 - sigma))).astype(jnp.bfloat16)
        up_grad = (back_hidden * (gate_act * sigma)).astype(jnp.bfloat16)
        in_grad = jnp.dot(gate_grad, gate_w.T, preferred_element_type=jnp.float32) + jnp.dot(up_grad, up_w.T, preferred_element_type=jnp.float32)
        grad_gate = add_at(grad_gate, expert, jnp.dot(rows_x.T, gate_grad, preferred_element_type=jnp.float32))
        grad_up = add_at(grad_up, expert, jnp.dot(rows_x.T, up_grad, preferred_element_type=jnp.float32))
        grad_down = add_at(grad_down, expert, jnp.dot(hidden.T, rows_dout, preferred_element_type=jnp.float32))
        return (grad_gate, grad_up, grad_down), (slot_prob[:, None] * partial_out, in_grad)

    start = (jnp.zeros(w_gate.shape, jnp.float32), jnp.zeros(w_up.shape, jnp.float32), jnp.zeros(w_down.shape, jnp.float32))
    grads, stacked = lax.scan(one_block, start, jnp.arange(nblocks, dtype=jnp.int32))
    output = stacked[0].reshape(-1, width)[token_slot].astype(jnp.bfloat16)
    input_grad = stacked[1].reshape(-1, width)[token_slot].astype(jnp.bfloat16)
    return (output, input_grad, grads[0], grads[1], grads[2])
```

```python
import functools

import jax
import jax.numpy as jnp
from jax import lax
from jax.experimental import pallas as pl
from jax.experimental.pallas import tpu as pltpu
from jax.sharding import PartitionSpec as P

EXP = 2
NZ = 4
CHUNK = 256
MESH = pl.DeviceIdType.MESH
LAG = 1


def wgrad_kernel(
    nx, fac, xst, out, gbuf, xbuf, psend, prec, pacc, g_send, g_recv, x_send, x_recv, z_send, z_recv
):
    ng = 2 * nx
    nq = fac.shape[0]
    me = lax.axis_index("dp")
    z = me // ng
    slot = me % ng
    xi = slot // 2
    core = slot % 2
    other = z * ng + xi * 2 + (1 - core)

    barrier = pltpu.get_barrier_semaphore()
    for d in range(1, ng):
        peer = z * ng + (slot + d) % ng
        pl.semaphore_signal(barrier, inc=1, device_id={"dp": peer}, device_id_type=MESH)
    for d in range(1, NZ):
        peer = ((z + d) % NZ) * ng + slot
        pl.semaphore_signal(barrier, inc=1, device_id={"dp": peer}, device_id_type=MESH)
    pl.semaphore_wait(barrier, ng - 1 + NZ - 1)

    def remote(src, dst, send, recv, peer):
        return pltpu.make_async_remote_copy(
            src_ref=src,
            dst_ref=dst,
            send_sem=send,
            recv_sem=recv,
            device_id={"dp": peer},
            device_id_type=MESH,
        )

    def x_copy(d):
        to = (slot + d) % ng
        return remote(xst.at[to], xbuf.at[slot], x_send.at[d], x_recv.at[slot], z * ng + to)

    def x_arrival(d):
        s = (slot + d) % ng
        return remote(xst.at[s], xbuf.at[s], x_send.at[d], x_recv.at[s], z * ng + s)

    def g_copy(q, k):
        peer = other if k == 0 else z * ng + ((xi + k) % nx) * 2 + core
        return remote(fac.at[q], gbuf.at[q, slot], g_send.at[q, k], g_recv.at[q, slot], peer)

    def g_forward(q, k):
        s = ((xi + k) % nx) * 2 + core
        return remote(
            gbuf.at[q, s], gbuf.at[q, s], g_send.at[q, nx - 1 + k], g_recv.at[q, s], other
        )

    def g_arrival(q, s):
        return remote(gbuf.at[q, s], gbuf.at[q, s], g_send.at[q, 0], g_recv.at[q, s], other)

    def z_copy(q, d):
        to = (z + d) % NZ
        return remote(
            psend.at[q, to], prec.at[q, z], z_send.at[q, d], z_recv.at[q, z], to * ng + slot
        )

    def z_arrival(q, d):
        s = (z + d) % NZ
        return remote(
            psend.at[q, s], prec.at[q, s], z_send.at[q, d], z_recv.at[q, s], s * ng + slot
        )

    for d in range(1, ng):
        x_copy(d).start()

    def send_own(q, carry):
        for k in range(nx):
            g_copy(q, k).start()
        return carry

    lax.fori_loop(0, nq, send_own, 0)
    xbuf[slot] = xst[slot]
    for d in range(1, ng):
        x_arrival(d).wait_recv()

    def forward(q):
        for k in range(1, nx):
            g_arrival(q, ((xi + k) % nx) * 2 + core).wait_recv()
            g_forward(q, k).start()

    def compute(q):
        gbuf[q, slot] = fac[q]
        for k in range(nx):
            g_arrival(q, ((xi + k) % nx) * 2 + (1 - core)).wait_recv()
        side = (q % 3) // 2
        part = jnp.dot(xbuf[0, side], gbuf[q, 0], preferred_element_type=jnp.float32)
        for s in range(1, ng):
            part = part + jnp.dot(xbuf[s, side], gbuf[q, s], preferred_element_type=jnp.float32)
        part = part.reshape(pacc.shape)
        pacc[...] = part
        psend[q] = part.astype(jnp.bfloat16)
        for d in range(1, NZ):
            z_copy(q, d).start()
        out[q] = pacc[z]

    for q in range(LAG):
        forward(q)

    def step(q, carry):
        forward(q + LAG)
        compute(q)
        return carry

    lax.fori_loop(0, nq - LAG, step, 0)

    def last(q, carry):
        compute(q)
        return carry

    lax.fori_loop(nq - LAG, nq, last, 0)

    def finish(q, carry):
        total = out[q]
        for d in range(1, NZ):
            z_arrival(q, d).wait_recv()
            total = total + prec[q, (z + d) % NZ].astype(jnp.float32)
        out[q] = total
        for k in range(nx):
            g_copy(q, k).wait_send()
        for k in range(1, nx):
            g_forward(q, k).wait_send()
        for d in range(1, NZ):
            z_copy(q, d).wait_send()
        return carry

    lax.fori_loop(0, nq, finish, 0)
    for d in range(1, ng):
        x_copy(d).wait_send()


def weight_grads(nx, fac, xst):
    nq, rows, chunk = fac.shape
    ng = 2 * nx
    own = xst.shape[2] // NZ
    vmem = pl.BlockSpec(memory_space=pltpu.VMEM)
    flops = 2 * nq * ng * rows * chunk * xst.shape[2]
    return pl.pallas_call(
        functools.partial(wgrad_kernel, nx),
        out_shape=jax.ShapeDtypeStruct((nq, own, chunk), jnp.float32),
        in_specs=[vmem, vmem],
        out_specs=vmem,
        scratch_shapes=[
            pltpu.VMEM((nq, ng, rows, chunk), jnp.bfloat16),
            pltpu.VMEM(xst.shape, jnp.bfloat16),
            pltpu.VMEM((nq, NZ, own, chunk), jnp.bfloat16),
            pltpu.VMEM((nq, NZ, own, chunk), jnp.bfloat16),
            pltpu.VMEM((NZ, own, chunk), jnp.float32),
            pltpu.SemaphoreType.DMA((nq, 2 * nx)),
            pltpu.SemaphoreType.DMA((nq, ng)),
            pltpu.SemaphoreType.DMA((ng,)),
            pltpu.SemaphoreType.DMA((ng,)),
            pltpu.SemaphoreType.DMA((nq, NZ)),
            pltpu.SemaphoreType.DMA((nq, NZ)),
        ],
        compiler_params=pltpu.CompilerParams(
            collective_id=0, has_side_effects=True, vmem_limit_bytes=56 * 1024 * 1024
        ),
        cost_estimate=pl.CostEstimate(
            flops=flops, bytes_accessed=400_000_000, transcendentals=0
        ),
    )(fac, xst)


def per_device(dp, tokens, cotangent, assign, prob, w_gate, w_up, w_down):
    width = tokens.shape[1]
    local_ff = w_gate.shape[2]
    nx = dp // (2 * NZ)
    ng = 2 * nx
    own = width // dp
    nc = local_ff // CHUNK
    f32, bf16 = jnp.float32, jnp.bfloat16

    both = lax.all_gather(jnp.stack([tokens, cotangent]), "shard", axis=1, tiled=True)
    x, dout = both[0], both[1]
    rows = x.shape[0]
    scaled = (prob[:, None] * dout.astype(f32)).astype(bf16)
    live = [(assign == e)[:, None] for e in range(EXP)]
    zero = jnp.zeros((), bf16)
    xs = [jnp.where(m, x, zero) for m in live]
    gs = [jnp.where(m, scaled, zero) for m in live]

    def pick(terms):
        total = terms[-1]
        for e in range(EXP - 1):
            total = jnp.where(live[e], terms[e], total)
        return total

    xcat = jnp.concatenate(xs, axis=1)
    gate = jnp.dot(xcat, w_gate.reshape(EXP * width, local_ff), preferred_element_type=f32)
    up = jnp.dot(xcat, w_up.reshape(EXP * width, local_ff), preferred_element_type=f32)
    back = sum(
        lax.dot_general(gs[e], w_down[e], (((1,), (1,)), ((), ())), preferred_element_type=f32)
        for e in range(EXP)
    )
    sigma = jax.nn.sigmoid(gate)
    act = gate * sigma
    hidden = (act * up).astype(bf16)
    gate_grad = (back * up * sigma * (1.0 + gate * (1.0 - sigma))).astype(bf16)
    up_grad = (back * act).astype(bf16)

    fac = jnp.stack([gate_grad, up_grad, hidden])
    fac = fac.reshape(3, rows, nc, CHUNK).transpose(2, 0, 1, 3).reshape(3 * nc, rows, CHUNK)
    xst = jnp.stack([jnp.stack(xs), jnp.stack(gs)])
    xst = xst.reshape(2, EXP, rows, NZ, ng, own).transpose(4, 0, 3, 1, 5, 2)
    xst = xst.reshape(ng, 2, NZ * EXP * own, rows)
    grads = weight_grads(nx, fac, xst).reshape(nc, 3, EXP, own, CHUNK)
    grad_gate = grads[:, 0].transpose(1, 2, 0, 3).reshape(EXP, own, local_ff)
    grad_up = grads[:, 1].transpose(1, 2, 0, 3).reshape(EXP, own, local_ff)
    grad_down = grads[:, 2].transpose(1, 0, 3, 2).reshape(EXP, local_ff, own)

    part_out = pick([jnp.dot(hidden, w_down[e], preferred_element_type=f32) for e in range(EXP)])
    contract = (((1,), (1,)), ((), ()))
    part_in = pick(
        [
            lax.dot_general(gate_grad, w_gate[e], contract, preferred_element_type=f32)
            + lax.dot_general(up_grad, w_up[e], contract, preferred_element_type=f32)
            for e in range(EXP)
        ]
    )
    sums = lax.psum_scatter(
        jnp.stack([part_out * prob[:, None], part_in]), "shard", scatter_dimension=1, tiled=True
    ).astype(bf16)
    return (sums[0], sums[1], grad_gate, grad_up, grad_down)


def solution(mesh):
    placed = (
        P(("dp", "shard"), None),
        P(("dp", "shard"), None),
        P("dp"),
        P("dp"),
        P(None, None, "shard"),
        P(None, None, "shard"),
        P(None, "shard", None),
    )
    return jax.shard_map(
        functools.partial(per_device, mesh.shape["dp"]),
        mesh=mesh,
        in_specs=placed,
        out_specs=(
            P(("dp", "shard"), None),
            P(("dp", "shard"), None),
            P(None, "dp", "shard"),
            P(None, "dp", "shard"),
            P(None, "shard", "dp"),
        ),
        check_vma=False,
    )
```

```python
import functools

import jax
import jax.numpy as jnp
from jax import lax
from jax.experimental import pallas as pl
from jax.experimental.pallas import tpu as pltpu
from jax.sharding import PartitionSpec as P

EXP = 2
NZ = 4
CHUNK = 256
MESH = pl.DeviceIdType.MESH
LAG = 1


def wgrad_kernel(
    nx, fac, xst, out, gbuf, xbuf, psend, prec, pacc, g_send, g_recv, x_send, x_recv, z_send, z_recv
):
    ng = 2 * nx
    nq = fac.shape[0]
    me = lax.axis_index("dp")
    z = me // ng
    slot = me % ng
    xi = slot // 2
    core = slot % 2
    other = z * ng + xi * 2 + (1 - core)

    barrier = pltpu.get_barrier_semaphore()
    for d in range(1, ng):
        peer = z * ng + (slot + d) % ng
        pl.semaphore_signal(barrier, inc=1, device_id={"dp": peer}, device_id_type=MESH)
    for d in range(1, NZ):
        peer = ((z + d) % NZ) * ng + slot
        pl.semaphore_signal(barrier, inc=1, device_id={"dp": peer}, device_id_type=MESH)
    pl.semaphore_wait(barrier, ng - 1 + NZ - 1)

    def remote(src, dst, send, recv, peer):
        return pltpu.make_async_remote_copy(
            src_ref=src,
            dst_ref=dst,
            send_sem=send,
            recv_sem=recv,
            device_id={"dp": peer},
            device_id_type=MESH,
        )

    def x_copy(d):
        to = (slot + d) % ng
        return remote(xst.at[to], xbuf.at[slot], x_send.at[d], x_recv.at[slot], z * ng + to)

    def x_arrival(d):
        s = (slot + d) % ng
        return remote(xst.at[s], xbuf.at[s], x_send.at[d], x_recv.at[s], z * ng + s)

    def g_copy(q, k):
        peer = other if k == 0 else z * ng + ((xi + k) % nx) * 2 + core
        return remote(fac.at[q], gbuf.at[q, slot], g_send.at[q, k], g_recv.at[q, slot], peer)

    def g_forward(q, k):
        s = ((xi + k) % nx) * 2 + core
        return remote(
            gbuf.at[q, s], gbuf.at[q, s], g_send.at[q, nx - 1 + k], g_recv.at[q, s], other
        )

    def g_arrival(q, s):
        return remote(gbuf.at[q, s], gbuf.at[q, s], g_send.at[q, 0], g_recv.at[q, s], other)

    def z_copy(q, d):
        to = (z + d) % NZ
        return remote(
            psend.at[q, to], prec.at[q, z], z_send.at[q, d], z_recv.at[q, z], to * ng + slot
        )

    def z_arrival(q, d):
        s = (z + d) % NZ
        return remote(
            psend.at[q, s], prec.at[q, s], z_send.at[q, d], z_recv.at[q, s], s * ng + slot
        )

    for d in range(1, ng):
        x_copy(d).start()

    def send_own(q, carry):
        for k in range(nx):
            g_copy(q, k).start()
        return carry

    lax.fori_loop(0, nq, send_own, 0)
    xbuf[slot] = xst[slot]
    for d in range(1, ng):
        x_arrival(d).wait_recv()

    def forward(q):
        for k in range(1, nx):
            g_arrival(q, ((xi + k) % nx) * 2 + core).wait_recv()
            g_forward(q, k).start()

    def compute(q):
        gbuf[q, slot] = fac[q]
        for k in range(nx):
            g_arrival(q, ((xi + k) % nx) * 2 + (1 - core)).wait_recv()
        side = (q % 3) // 2
        part = jnp.dot(xbuf[0, side], gbuf[q, 0], preferred_element_type=jnp.float32)
        for s in range(1, ng):
            part = part + jnp.dot(xbuf[s, side], gbuf[q, s], preferred_element_type=jnp.float32)
        part = part.reshape(pacc.shape)
        pacc[...] = part
        psend[q] = part.astype(jnp.bfloat16)
        for d in range(1, NZ):
            z_copy(q, d).start()
        out[q] = pacc[z]

    for q in range(LAG):
        forward(q)

    def step(q, carry):
        forward(q + LAG)
        compute(q)
        return carry

    lax.fori_loop(0, nq - LAG, step, 0)

    def last(q, carry):
        compute(q)
        return carry

    lax.fori_loop(nq - LAG, nq, last, 0)

    def finish(q, carry):
        total = out[q]
        for d in range(1, NZ):
            z_arrival(q, d).wait_recv()
            total = total + prec[q, (z + d) % NZ].astype(jnp.float32)
        out[q] = total
        for k in range(nx):
            g_copy(q, k).wait_send()
        for k in range(1, nx):
            g_forward(q, k).wait_send()
        for d in range(1, NZ):
            z_copy(q, d).wait_send()
        return carry

    lax.fori_loop(0, nq, finish, 0)
    for d in range(1, ng):
        x_copy(d).wait_send()


def weight_grads(nx, fac, xst):
    nq, rows, chunk = fac.shape
    ng = 2 * nx
    own = xst.shape[2] // NZ
    vmem = pl.BlockSpec(memory_space=pltpu.VMEM)
    flops = 2 * nq * ng * rows * chunk * xst.shape[2]
    return pl.pallas_call(
        functools.partial(wgrad_kernel, nx),
        out_shape=jax.ShapeDtypeStruct((nq, own, chunk), jnp.float32),
        in_specs=[vmem, vmem],
        out_specs=vmem,
        scratch_shapes=[
            pltpu.VMEM((nq, ng, rows, chunk), jnp.bfloat16),
            pltpu.VMEM(xst.shape, jnp.bfloat16),
            pltpu.VMEM((nq, NZ, own, chunk), jnp.bfloat16),
            pltpu.VMEM((nq, NZ, own, chunk), jnp.bfloat16),
            pltpu.VMEM((NZ, own, chunk), jnp.float32),
            pltpu.SemaphoreType.DMA((nq, 2 * nx)),
            pltpu.SemaphoreType.DMA((nq, ng)),
            pltpu.SemaphoreType.DMA((ng,)),
            pltpu.SemaphoreType.DMA((ng,)),
            pltpu.SemaphoreType.DMA((nq, NZ)),
            pltpu.SemaphoreType.DMA((nq, NZ)),
        ],
        compiler_params=pltpu.CompilerParams(
            collective_id=0, has_side_effects=True, vmem_limit_bytes=56 * 1024 * 1024
        ),
        cost_estimate=pl.CostEstimate(
            flops=flops, bytes_accessed=400_000_000, transcendentals=0
        ),
    )(fac, xst)


def per_device(dp, shards, tokens, cotangent, assign, prob, w_gate, w_up, w_down):
    width = tokens.shape[1]
    local_ff = w_gate.shape[2]
    nx = dp // (2 * NZ)
    ng = 2 * nx
    own = width // dp
    nc = local_ff // CHUNK
    f32, bf16 = jnp.float32, jnp.bfloat16

    mine = jnp.stack([tokens, cotangent])
    block = mine.shape[1]
    at = lax.axis_index("shard")
    both = jnp.zeros((2, shards * block, width), bf16)
    both = lax.dynamic_update_slice_in_dim(both, mine, at * block, 1)
    for hop in range(1, shards):
        got = lax.ppermute(mine, "shard", [(i, (i + hop) % shards) for i in range(shards)])
        both = lax.dynamic_update_slice_in_dim(both, got, ((at - hop) % shards) * block, 1)
    x, dout = both[0], both[1]
    rows = x.shape[0]
    scaled = (prob[:, None] * dout.astype(f32)).astype(bf16)
    live = [(assign == e)[:, None] for e in range(EXP)]
    zero = jnp.zeros((), bf16)
    xs = [jnp.where(m, x, zero) for m in live]
    gs = [jnp.where(m, scaled, zero) for m in live]

    def pick(terms):
        total = terms[-1]
        for e in range(EXP - 1):
            total = jnp.where(live[e], terms[e], total)
        return total

    xcat = jnp.concatenate(xs, axis=1)
    gate = jnp.dot(xcat, w_gate.reshape(EXP * width, local_ff), preferred_element_type=f32)
    up = jnp.dot(xcat, w_up.reshape(EXP * width, local_ff), preferred_element_type=f32)
    back = sum(
        lax.dot_general(gs[e], w_down[e], (((1,), (1,)), ((), ())), preferred_element_type=f32)
        for e in range(EXP)
    )
    sigma = jax.nn.sigmoid(gate)
    act = gate * sigma
    hidden = (act * up).astype(bf16)
    gate_grad = (back * up * sigma * (1.0 + gate * (1.0 - sigma))).astype(bf16)
    up_grad = (back * act).astype(bf16)

    fac = jnp.stack([gate_grad, up_grad, hidden])
    fac = fac.reshape(3, rows, nc, CHUNK).transpose(2, 0, 1, 3).reshape(3 * nc, rows, CHUNK)
    xst = jnp.stack([jnp.stack(xs), jnp.stack(gs)])
    xst = xst.reshape(2, EXP, rows, NZ, ng, own).transpose(4, 0, 3, 1, 5, 2)
    xst = xst.reshape(ng, 2, NZ * EXP * own, rows)
    grads = weight_grads(nx, fac, xst).reshape(nc, 3, EXP, own, CHUNK)
    grad_gate = grads[:, 0].transpose(1, 2, 0, 3).reshape(EXP, own, local_ff)
    grad_up = grads[:, 1].transpose(1, 2, 0, 3).reshape(EXP, own, local_ff)
    grad_down = grads[:, 2].transpose(1, 0, 3, 2).reshape(EXP, local_ff, own)

    part_out = pick([jnp.dot(hidden, w_down[e], preferred_element_type=f32) for e in range(EXP)])
    contract = (((1,), (1,)), ((), ()))
    part_in = pick(
        [
            lax.dot_general(gate_grad, w_gate[e], contract, preferred_element_type=f32)
            + lax.dot_general(up_grad, w_up[e], contract, preferred_element_type=f32)
            for e in range(EXP)
        ]
    )
    sums = lax.psum_scatter(
        jnp.stack([part_out * prob[:, None], part_in]), "shard", scatter_dimension=1, tiled=True
    ).astype(bf16)
    return (sums[0], sums[1], grad_gate, grad_up, grad_down)


def solution(mesh):
    placed = (
        P(("dp", "shard"), None),
        P(("dp", "shard"), None),
        P("dp"),
        P("dp"),
        P(None, None, "shard"),
        P(None, None, "shard"),
        P(None, "shard", None),
    )
    return jax.shard_map(
        functools.partial(per_device, mesh.shape["dp"], mesh.shape["shard"]),
        mesh=mesh,
        in_specs=placed,
        out_specs=(
            P(("dp", "shard"), None),
            P(("dp", "shard"), None),
            P(None, "dp", "shard"),
            P(None, "dp", "shard"),
            P(None, "shard", "dp"),
        ),
        check_vma=False,
    )
```
